32 devices in a mesh: seq: 16 (over z, y, x), kv: 2 (over core).
Axes of the slice: x: 2, y: 2, z: 4, core: 2. Of those that a mesh axis runs over, the one named last changes fastest.
Arguments:
- text_query: bfloat16 [2048, 2048], P('seq', 'kv'), may hold values from -20 to 20, as said below
- vision_key: bfloat16 [512, 256], P('seq', 'kv'), may hold values from -4 to 4, as said below
- vision_value: bfloat16 [512, 256], P('seq', 'kv'), may hold values from -6 to 6
- grad_output: bfloat16 [2048, 2048], P('seq', 'kv'), may hold values from -192 to 192
- key_weight: bfloat16 [8192, 256], P('seq', 'kv'), may hold values from -0.09375 to 0.09375
- value_weight: bfloat16 [8192, 256], P('seq', 'kv'), may hold values from -0.09375 to 0.09375
Outputs:
- grad_query: bfloat16 [2048, 2048], P('seq', 'kv')
- grad_vision: bfloat16 [512, 8192], P('seq', 'kv')
The draws below stay inside these ranges and needn't reach their ends.
Inputs may be any that keep to these rules, and one draw needn't show every extreme that they name: `text_query`: entries of order one; some rows of single heads may be large multiples of a key row. `vision_key`: entries of order one.
All inputs are finite; a program needn't handle non-finite values.
Results may differ from the reference program's by a relative error of at most 0.02.
Values may be sent and summed in bfloat16 or wider, within the bound.
No kernel may reach another device: no remote copies, remote signals or barrier semaphores. Data moves between devices by JAX's collectives and lax.ppermute only.
A program may use at most 64 MiB of HBM per device.

```python
import math
import jax
import jax.numpy as jnp
from jax import lax

HEAD = 128
QPG = 8
VIS_WIDTH = 8192
KV_HEADS = 2
Q_HEADS = 16
TEXT = 2048
VISION = 512


def structure(key):
    folded = jax.random.fold_in(key, 11)
    key_query, key_keys = jax.random.split(folded, 2)
    queries = jnp.clip(jax.random.normal(key_query, (TEXT, Q_HEADS * HEAD), jnp.float32), -4.0, 4.0)
    keys_all = jnp.clip(jax.random.normal(key_keys, (VISION, KV_HEADS * HEAD), jnp.float32), -4.0, 4.0)
    return (queries, keys_all)


def draw_text_query(key, part):
    return structure(key)[0].astype(jnp.bfloat16)


def draw_vision_key(key, part):
    return structure(key)[1].astype(jnp.bfloat16)


def spiked(entries, own_key, source, target, parts, factor):
    owner, partner = [(jnp.arange(entries.shape[position]) // (entries.shape[position] // parts)).reshape([-1 if axis == position else 1 for axis in range(entries.ndim)]) for position in (source, target)]
    chosen = jax.random.permutation(own_key, parts)[partner]
    strong = (owner == chosen) | (owner == (partner + parts // 2) % parts)
    return jnp.where(strong, factor * entries, entries)


def levels(key, shape, shards, least, top_value):
    gain = 1.0
    for axis_at, blocks in shards:
        steps = jax.random.uniform(jax.random.fold_in(jax.random.fold_in(key, 6), axis_at), (blocks,), jnp.float32, least / len(shards), top_value / len(shards))
        gain = gain * jnp.repeat(jnp.exp(steps), shape[axis_at] // blocks).reshape((-1,) + (1,) * (len(shape) - 1 - axis_at))
    return gain


def gaussian(rng, dims, spread, most, cuts=(), held_as=jnp.bfloat16):
    loudness = levels(rng, dims, cuts, -0.22, 0.18) if cuts else 1.0
    result = jax.random.normal(rng, dims, jnp.float32) * spread * loudness
    return jnp.minimum(jnp.maximum(result, -most), most).astype(held_as)


def noise_with(own_key, extent, width, most, shards, heavy, kind=jnp.bfloat16):
    drawn = width * jax.random.normal(own_key, extent, jnp.float32)
    if shards:
        drawn = drawn * levels(own_key, extent, shards, -0.22, 0.18)
    return jnp.clip(spiked(drawn, jax.random.fold_in(own_key, 3), *heavy), -most, most).astype(kind)


def setup_inputs(seed: int = 0) -> dict:
    key_list = jax.random.split(jax.random.key(seed), 7)
    return {
        "text_query": draw_text_query(jax.random.fold_in(key_list[6], 71), 0),
        "vision_key": draw_vision_key(jax.random.fold_in(key_list[6], 71), 0),
        "vision_value": gaussian(key_list[2], (VISION, KV_HEADS * HEAD), 1.0, 6.0, ((0, 16), (1, 2))),
        "grad_output": gaussian(key_list[3], (TEXT, Q_HEADS * HEAD), 32.0, 192.0, ((0, 16), (1, 2))),
        "key_weight": noise_with(key_list[4], (VIS_WIDTH, KV_HEADS * HEAD), VIS_WIDTH ** -0.5, 0.09375, ((0, 16), (1, 2)), (1, 0, 16, 2.0)),
        "value_weight": noise_with(key_list[5], (VIS_WIDTH, KV_HEADS * HEAD), VIS_WIDTH ** -0.5, 0.09375, ((0, 16), (1, 2)), (1, 0, 16, 2.0)),
    }


def reference(text_query, vision_key, vision_value, grad_output, key_weight, value_weight):
    scaling = 1.0 / math.sqrt(HEAD)
    query_heads = text_query.reshape(TEXT, Q_HEADS, HEAD).transpose(1, 0, 2)
    output_heads = grad_output.reshape(TEXT, Q_HEADS, HEAD).transpose(1, 0, 2)
    key_heads = vision_key.reshape(VISION, KV_HEADS, HEAD).transpose(1, 0, 2)
    value_heads = vision_value.reshape(VISION, KV_HEADS, HEAD).transpose(1, 0, 2)
    group_ids = (jnp.arange(Q_HEADS, dtype=jnp.int32) // QPG).astype(jnp.int32)

    def single_head(inputs):
        query_one, output_one, group_id = inputs
        key_one = lax.dynamic_index_in_dim(key_heads, group_id, 0, keepdims=False)
        value_one = lax.dynamic_index_in_dim(value_heads, group_id, 0, keepdims=False)
        logits = jnp.dot(query_one, key_one.T, preferred_element_type=jnp.float32) * scaling
        row_max = lax.optimization_barrier(jnp.max(logits, axis=1, keepdims=True))
        exponent = jnp.exp(logits - row_max)
        row_sums = lax.optimization_barrier(jnp.sum(exponent, axis=1, keepdims=True))
        attention = exponent / row_sums
        grad_probs = jnp.dot(output_one, value_one.T, preferred_element_type=jnp.float32)
        row_dots = lax.optimization_barrier(jnp.sum(attention * grad_probs, axis=1, keepdims=True))
        value_term = jnp.dot(attention.astype(jnp.bfloat16).T, output_one, preferred_element_type=jnp.float32)
        grad_logits = (attention * (grad_probs - row_dots) * scaling).astype(jnp.bfloat16)
        query_term = jnp.dot(grad_logits, key_one, preferred_element_type=jnp.float32).astype(jnp.bfloat16)
        key_term = jnp.dot(grad_logits.T, query_one, preferred_element_type=jnp.float32)
        return (query_term, key_term, value_term)
    query_terms, key_terms, value_terms = lax.map(single_head, (query_heads, output_heads, group_ids))
    grad_query = query_terms.transpose(1, 0, 2).reshape(TEXT, Q_HEADS * HEAD)
    grad_key = key_terms.reshape(KV_HEADS, QPG, VISION, HEAD).sum(axis=1)
    grad_key = grad_key.transpose(1, 0, 2).reshape(VISION, KV_HEADS * HEAD).astype(jnp.bfloat16)
    grad_value = value_terms.reshape(KV_HEADS, QPG, VISION, HEAD).sum(axis=1)
    grad_value = grad_value.transpose(1, 0, 2).reshape(VISION, KV_HEADS * HEAD).astype(jnp.bfloat16)
    grad_vision = jnp.dot(grad_key, key_weight.T, preferred_element_type=jnp.float32)
    grad_vision = grad_vision + jnp.dot(grad_value, value_weight.T, preferred_element_type=jnp.float32)
    return (grad_query, grad_vision.astype(jnp.bfloat16))
```

```python
import math

import jax
import jax.numpy as jnp
from jax import lax
from jax.sharding import PartitionSpec as P

HEAD = 128


def exchange(block, axis, size, distance):
    return lax.ppermute(block, axis, [(i, i ^ distance) for i in range(size)])


def gather_cube(block, cube):
    blocks = [block]
    if cube >= 4:
        blocks += [exchange(block, "seq", 2 * cube, d) for d in (1, 2, 3)]
    while len(blocks) < cube:
        distance = len(blocks)
        moved = exchange(jnp.stack(blocks), "seq", 2 * cube, distance)
        blocks += [moved[i] for i in range(distance)]
    return jnp.stack(blocks)


def attention_terms(queries, upstream, keys, values):
    scaling = 1.0 / math.sqrt(HEAD)
    rows = queries.shape[0]
    heads = queries.shape[1] // HEAD
    queries = queries.reshape(rows, heads, HEAD)
    upstream = upstream.reshape(rows, heads, HEAD)
    f32 = jnp.float32
    logits = jnp.einsum("thd,kd->htk", queries, keys, preferred_element_type=f32) * scaling
    grad_probs = jnp.einsum("thd,kd->htk", upstream, values, preferred_element_type=f32)
    exponent = jnp.exp(logits - jnp.max(logits, axis=2, keepdims=True))
    attention = exponent / jnp.sum(exponent, axis=2, keepdims=True)
    row_dots = jnp.sum(attention * grad_probs, axis=2, keepdims=True)
    grad_logits = (attention * (grad_probs - row_dots) * scaling).astype(jnp.bfloat16)
    attention_low = attention.astype(jnp.bfloat16)
    grad_query = jnp.einsum("htk,kd->thd", grad_logits, keys, preferred_element_type=f32)
    key_term = jnp.einsum("htk,thd->kd", grad_logits, queries, preferred_element_type=f32)
    value_term = jnp.einsum("htk,thd->kd", attention_low, upstream, preferred_element_type=f32)
    terms = jnp.concatenate([key_term, value_term], axis=1).astype(jnp.bfloat16)
    return grad_query.reshape(rows, heads * HEAD).astype(jnp.bfloat16), terms


def shards(text_query, vision_key, vision_value, grad_output, key_weight, value_weight):
    chips = lax.axis_size("seq")
    cores = lax.axis_size("kv")
    cube = chips // 2
    half = cores // 2
    me = lax.axis_index("seq")
    core = lax.axis_index("kv")
    groups = [list(range(cube)), list(range(cube, chips))]
    own = vision_key.shape[0]
    weights = gather_cube(jnp.concatenate([key_weight, value_weight], axis=1), cube)

    pair = jnp.concatenate([vision_key, vision_value], axis=1)
    everyone = lax.all_to_all(
        jnp.broadcast_to(pair, (chips,) + pair.shape), "seq", 0, 0
    ).reshape(chips * own, 2 * HEAD)
    grad_query, terms = attention_terms(
        text_query, grad_output, everyone[:, :HEAD], everyone[:, HEAD:]
    )

    blocks = terms.reshape(2, cube, own, 2 * HEAD).transpose(1, 0, 2, 3)
    arrived = lax.all_to_all(blocks, "seq", 0, 0, axis_index_groups=groups)
    partial = jnp.sum(arrived.astype(jnp.float32), axis=0)
    grads = (partial + exchange(partial, "seq", chips, cube)).astype(jnp.bfloat16)

    product = jnp.einsum("qtc,drc->qdtr", grads, weights, preferred_element_type=jnp.float32)
    place = (me % cube) ^ jnp.arange(cube)
    product = jnp.take(product, place, axis=1)
    columns = product.transpose(0, 2, 1, 3).reshape(2, own, half, -1).transpose(0, 2, 1, 3)
    columns = columns.reshape(cores, own, -1)
    total = lax.dynamic_index_in_dim(columns, core, 0, keepdims=False)
    for d in range(1, cores):
        other = lax.dynamic_index_in_dim(columns, core ^ d, 0, keepdims=False)
        total = total + exchange(other.astype(jnp.bfloat16), "kv", cores, d).astype(jnp.float32)
    total = total.astype(jnp.bfloat16)
    routes = [
        (u * cores + j, (u ^ cube) * cores + (j + half) % cores)
        for u in range(chips)
        for j in range(cores)
        if j // half != u // cube
    ]
    received = lax.ppermute(total, ("seq", "kv"), routes)
    grad_vision = jnp.where(core // half == me // cube, total, received)
    return (grad_query, grad_vision)


def solution(mesh):
    spec = P("seq", "kv")
    return jax.shard_map(
        shards,
        mesh=mesh,
        in_specs=(spec,) * 6,
        out_specs=(spec, spec),
        check_vma=False,
    )
```

```python
import functools
import math

import jax
import jax.numpy as jnp
from jax import lax
from jax.experimental import pallas as pl
from jax.experimental.pallas import tpu as pltpu
from jax.sharding import PartitionSpec as P

HEAD = 128
F32 = jnp.float32
BF16 = jnp.bfloat16
IN_VMEM = pl.BlockSpec(memory_space=pltpu.VMEM)
SIDE_BY_SIDE = (((1,), (1,)), ((), ()))
ON_TOP = (((0,), (0,)), ((), ()))


def exchange(block, axis, size, distance):
    return lax.ppermute(block, axis, [(i, i ^ distance) for i in range(size)])


def attention_kernel(queries_ref, upstream_ref, vision_ref, query_ref, terms_ref, rows, low):
    row_count, width = queries_ref.shape
    heads = width // HEAD
    scaling = 1.0 / math.sqrt(HEAD)
    keys = vision_ref[:, :HEAD]
    values = vision_ref[:, HEAD:]
    for h in range(heads):
        lanes = slice(h * HEAD, (h + 1) * HEAD)
        at = slice(h * row_count, (h + 1) * row_count)
        rows[0, at, :] = queries_ref[:, lanes]
        rows[1, at, :] = upstream_ref[:, lanes]
    step = 2 if heads % 2 == 0 else 1
    for h in range(0, heads, step):
        at = slice(h * row_count, (h + step) * row_count)
        logits = lax.dot_general(keys, rows[0, at, :], SIDE_BY_SIDE, preferred_element_type=F32)
        grad_probs = lax.dot_general(values, rows[1, at, :], SIDE_BY_SIDE, preferred_element_type=F32)
        top = jnp.max(logits, axis=0, keepdims=True)
        exponent = jnp.exp2((logits - top) * (scaling * math.log2(math.e)))
        inverse = 1.0 / jnp.sum(exponent, axis=0, keepdims=True)
        row_dots = jnp.sum(exponent * grad_probs, axis=0, keepdims=True) * inverse
        low[1, :, at] = (exponent * inverse).astype(BF16)
        grad_logits = (exponent * (grad_probs - row_dots) * (inverse * scaling)).astype(BF16)
        low[0, :, at] = grad_logits
        grad_query = lax.dot_general(grad_logits, keys, ON_TOP, preferred_element_type=F32)
        for i in range(step):
            lanes = slice((h + i) * HEAD, (h + i + 1) * HEAD)
            query_ref[:, lanes] = grad_query[i * row_count : (i + 1) * row_count].astype(BF16)
    plane, line, own, _ = terms_ref.shape
    for i in range(2):
        term = jnp.dot(low[i], rows[i], preferred_element_type=F32).astype(BF16)
        term = term.reshape(line, plane, own, HEAD)
        for p in range(plane):
            terms_ref[p, :, :, i * HEAD : (i + 1) * HEAD] = term[:, p]


def attention_terms(queries, upstream, vision, plane, line):
    rows, width = queries.shape
    tokens = vision.shape[0]
    pairs = rows * width // HEAD
    return pl.pallas_call(
        attention_kernel,
        out_shape=(
            jax.ShapeDtypeStruct((rows, width), BF16),
            jax.ShapeDtypeStruct((plane, line, tokens // (plane * line), 2 * HEAD), BF16),
        ),
        in_specs=[IN_VMEM] * 3,
        out_specs=(IN_VMEM, IN_VMEM),
        scratch_shapes=[
            pltpu.VMEM((2, pairs, HEAD), BF16),
            pltpu.VMEM((2, tokens, pairs), BF16),
        ],
        compiler_params=pltpu.CompilerParams(vmem_limit_bytes=48 * 1024 * 1024),
        cost_estimate=pl.CostEstimate(
            flops=10 * pairs * tokens * HEAD,
            bytes_accessed=8 * rows * width + 4 * tokens * HEAD,
            transcendentals=pairs * tokens,
        ),
        name="attention_terms",
    )(queries, upstream, vision)


def project_kernel(mine_ref, near_ref, far_ref, cross_ref, *refs):
    plane = (len(refs) - 3) // 2
    weights, (stay_ref, go_ref, grads) = refs[:-3], refs[-3:]
    me = lax.axis_index("seq")
    home = lax.axis_index("kv") == me // (2 * plane)
    odd = lax.rem(me // plane, 2)
    spot = lax.rem(me, plane)
    total = mine_ref[...] + near_ref[...].astype(F32) + far_ref[...].astype(F32)
    grads[...] = (total + cross_ref[...].astype(F32)).astype(BF16)
    stay = jnp.where(home, odd, 1 - odd)
    width = grads.shape[2] // 2
    rows = grads.shape[1]
    ordered = jnp.concatenate([grads[stay], grads[1 - stay]], axis=0)
    for d in range(plane):
        product = lax.dot_general(
            ordered[:, :width], weights[d][...], SIDE_BY_SIDE, preferred_element_type=F32
        )
        product += lax.dot_general(
            ordered[:, width:], weights[plane + d][...], SIDE_BY_SIDE, preferred_element_type=F32
        )
        columns = weights[d].shape[0]
        at = pl.ds(pl.multiple_of(jnp.bitwise_xor(spot, d) * columns, columns), columns)
        stay_ref[:, at] = product[:rows].astype(BF16)
        go_ref[:, at] = product[rows:].astype(BF16)


def project(mine, arrived, weights):
    rows = mine.shape[1]
    plane = len(weights) // 2
    columns = plane * weights[0].shape[0]
    shape = jax.ShapeDtypeStruct((rows, columns), BF16)
    return pl.pallas_call(
        project_kernel,
        out_shape=(shape, shape),
        in_specs=[IN_VMEM] * (4 + len(weights)),
        out_specs=(IN_VMEM, IN_VMEM),
        scratch_shapes=[pltpu.VMEM(mine.shape, BF16)],
        compiler_params=pltpu.CompilerParams(vmem_limit_bytes=32 * 1024 * 1024),
        cost_estimate=pl.CostEstimate(
            flops=8 * rows * columns * 2 * HEAD, bytes_accessed=8 * columns * HEAD, transcendentals=0
        ),
        name="project",
    )(mine, *arrived, *weights)


def gather_cube(block, cube):
    blocks = [block]
    while len(blocks) < cube:
        distance = len(blocks)
        moved = exchange(jnp.stack(blocks), "seq", 2 * cube, distance)
        blocks += [moved[i] for i in range(distance)]
    return jnp.stack(blocks)


def many_cores(text_query, vision_key, vision_value, grad_output, key_weight, value_weight):
    chips = lax.axis_size("seq")
    cores = lax.axis_size("kv")
    cube = chips // 2
    half = cores // 2
    me = lax.axis_index("seq")
    core = lax.axis_index("kv")
    groups = [list(range(cube)), list(range(cube, chips))]
    own = vision_key.shape[0]
    weights = gather_cube(jnp.concatenate([key_weight, value_weight], axis=1), cube)
    pair = jnp.concatenate([vision_key, vision_value], axis=1)
    vision = lax.all_to_all(jnp.broadcast_to(pair, (chips,) + pair.shape), "seq", 0, 0)
    grad_query, terms = attention_terms(
        text_query, grad_output, vision.reshape(chips * own, 2 * HEAD), cube, 2
    )
    arrived = lax.all_to_all(terms, "seq", 0, 0, axis_index_groups=groups)
    partial = jnp.sum(arrived.astype(F32), axis=0)
    grads = (partial + exchange(partial, "seq", chips, cube)).astype(BF16)
    product = jnp.einsum("qtc,drc->qdtr", grads, weights, preferred_element_type=F32)
    place = (me % cube) ^ jnp.arange(cube)
    product = jnp.take(product, place, axis=1)
    columns = product.transpose(0, 2, 1, 3).reshape(2, own, half, -1).transpose(0, 2, 1, 3)
    columns = columns.reshape(cores, own, -1)
    total = lax.dynamic_index_in_dim(columns, core, 0, keepdims=False)
    for d in range(1, cores):
        other = lax.dynamic_index_in_dim(columns, core ^ d, 0, keepdims=False)
        total = total + exchange(other.astype(BF16), "kv", cores, d).astype(F32)
    total = total.astype(BF16)
    routes = [
        (u * cores + j, (u ^ cube) * cores + (j + half) % cores)
        for u in range(chips)
        for j in range(cores)
        if j // half != u // cube
    ]
    received = lax.ppermute(total, ("seq", "kv"), routes)
    grad_vision = jnp.where(core // half == me // cube, total, received)
    return (grad_query, grad_vision)


def two_cores(text_query, vision_key, vision_value, grad_output, key_weight, value_weight):
    chips = lax.axis_size("seq")
    me = lax.axis_index("seq")
    core = lax.axis_index("kv")
    line = 4
    plane = chips // line
    own = vision_key.shape[0]

    pair = jnp.concatenate([vision_key, vision_value], axis=1)
    vision = lax.all_to_all(jnp.broadcast_to(pair, (chips,) + pair.shape), "seq", 0, 0)
    weight = jnp.concatenate([key_weight, value_weight], axis=1)
    weights = [weight] + [exchange(weight, "seq", chips, d) for d in range(1, plane)]
    grad_query, terms = attention_terms(
        text_query, grad_output, vision.reshape(chips * own, 2 * HEAD), plane, line
    )
    terms, weights[1:3] = lax.optimization_barrier((terms, weights[1:3]))
    weights += [exchange(w, "kv", 2, 1) for w in weights]

    groups = [list(range(z * plane, (z + 1) * plane)) for z in range(line)]
    arrived = lax.all_to_all(terms, "seq", 0, 0, axis_index_groups=groups)
    sums = jnp.sum(arrived.astype(F32), axis=0)
    mine = lax.dynamic_slice_in_dim(sums, 2 * core, 2, 0)
    yours = lax.dynamic_slice_in_dim(sums, 2 - 2 * core, 2, 0)
    mine = jnp.concatenate([mine, exchange(yours, "kv", 2, 1)], axis=2)
    near, far, cross = plane, 2 * plane, 3 * plane
    arrived = [exchange(mine.astype(BF16), "seq", chips, d) for d in (near, far, cross)]
    stay, go = project(mine, arrived, weights)

    routes_a, routes_b = [], []
    for u in range(chips):
        home = u // far
        routes_a.append((2 * u + home, 2 * (u ^ near) + home))
        routes_a.append((2 * u + 1 - home, 2 * (u ^ far) + home))
        routes_b.append((2 * u + 1 - home, 2 * (u ^ cross) + home))
    at_home = core == me // far
    first = lax.ppermute(go, ("seq", "kv"), routes_a)
    second = lax.ppermute(stay, ("seq", "kv"), routes_b)
    same = jnp.where(at_home, stay, first)
    other = jnp.where(at_home, first, second)
    upper = (me // near) % 2 == 1
    grad_vision = jnp.concatenate(
        [jnp.where(upper, other, same), jnp.where(upper, same, other)], axis=1
    )
    return (grad_query, grad_vision)


def solution(mesh):
    spec = P("seq", "kv")
    return jax.shard_map(
        two_cores if mesh.shape["kv"] == 2 and mesh.shape["seq"] % 4 == 0 else many_cores,
        mesh=mesh,
        in_specs=(spec,) * 6,
        out_specs=(spec, spec),
        check_vma=False,
    )
```

```python
import functools
import math

import jax
import jax.numpy as jnp
from jax import lax
from jax.experimental import pallas as pl
from jax.experimental.pallas import tpu as pltpu
from jax.sharding import PartitionSpec as P

HEAD = 128
F32 = jnp.float32
BF16 = jnp.bfloat16
IN_VMEM = pl.BlockSpec(memory_space=pltpu.VMEM)
SIDE_BY_SIDE = (((1,), (1,)), ((), ()))
ON_TOP = (((0,), (0,)), ((), ()))


def exchange(block, axis, size, distance):
    return lax.ppermute(block, axis, [(i, i ^ distance) for i in range(size)])


def spread_kernel(keys_ref, values_ref, out_ref):
    for i in range(out_ref.shape[0]):
        out_ref[i, :, :HEAD] = keys_ref[...]
        out_ref[i, :, HEAD:] = values_ref[...]


def spread(keys, values, copies):
    return pl.pallas_call(
        spread_kernel,
        out_shape=pltpu.VMEM((copies, keys.shape[0], 2 * HEAD), BF16),
        in_specs=[IN_VMEM] * 2,
        out_specs=IN_VMEM,
        name="spread",
    )(keys, values)


def attention_kernel(queries_ref, upstream_ref, vision_ref, low_ref, *refs):
    terms_refs, (rows, low, sums) = refs[:-3], refs[-3:]
    row_count, width = queries_ref.shape
    heads = width // HEAD
    scaling = 1.0 / math.sqrt(HEAD)
    keys = vision_ref[:, :HEAD]
    values = vision_ref[:, HEAD:]
    for h in range(heads):
        lanes = slice(h * HEAD, (h + 1) * HEAD)
        at = slice(h * row_count, (h + 1) * row_count)
        rows[0, at, :] = queries_ref[:, lanes]
        rows[1, at, :] = upstream_ref[:, lanes]
    step = 2 if heads % 2 == 0 else 1
    for h in range(0, heads, step):
        at = slice(h * row_count, (h + step) * row_count)
        logits = lax.dot_general(keys, rows[0, at, :], SIDE_BY_SIDE, preferred_element_type=F32)
        grad_probs = lax.dot_general(values, rows[1, at, :], SIDE_BY_SIDE, preferred_element_type=F32)
        top = jnp.max(logits, axis=0, keepdims=True)
        exponent = jnp.exp2((logits - top) * (scaling * math.log2(math.e)))
        inverse = 1.0 / jnp.sum(exponent, axis=0, keepdims=True)
        row_dots = jnp.sum(exponent * grad_probs, axis=0, keepdims=True) * inverse
        low[:, at] = (exponent * inverse).astype(BF16)
        low_ref[:, at] = (exponent * (grad_probs - row_dots) * (inverse * scaling)).astype(BF16)
    line, plane, own, _ = sums.shape
    for i, factor in enumerate((low_ref, low)):
        term = jnp.dot(factor[...], rows[i], preferred_element_type=F32)
        sums[:, :, :, i * HEAD : (i + 1) * HEAD] = term.reshape(line, plane, own, HEAD)
    spot = lax.rem(lax.axis_index("seq"), plane)
    for d, ref in enumerate(terms_refs):
        ref[...] = sums[:, jnp.bitwise_xor(spot, d)].astype(ref.dtype)


def attention_terms(queries, upstream, vision, plane, line):
    rows, width = queries.shape
    tokens = vision.shape[0]
    pairs = rows * width // HEAD
    own = tokens // (plane * line)
    low, *terms = pl.pallas_call(
        attention_kernel,
        out_shape=[jax.ShapeDtypeStruct((tokens, pairs), BF16)]
        + [
            jax.ShapeDtypeStruct((line, own, 2 * HEAD), BF16 if d else F32) for d in range(plane)
        ],
        in_specs=[IN_VMEM] * 3,
        out_specs=[IN_VMEM] * (1 + plane),
        scratch_shapes=[
            pltpu.VMEM((2, pairs, HEAD), BF16),
            pltpu.VMEM((tokens, pairs), BF16),
            pltpu.VMEM((line, plane, own, 2 * HEAD), F32),
        ],
        compiler_params=pltpu.CompilerParams(vmem_limit_bytes=48 * 1024 * 1024),
        cost_estimate=pl.CostEstimate(
            flops=8 * pairs * tokens * HEAD,
            bytes_accessed=4 * rows * width + 4 * tokens * HEAD,
            transcendentals=pairs * tokens,
        ),
        name="attention_terms",
    )(queries, upstream, vision)
    return low, terms


def query_kernel(low_ref, vision_ref, query_ref):
    rows = query_ref.shape[0]
    keys = vision_ref[:, :HEAD]
    for h in range(query_ref.shape[1] // HEAD):
        at = slice(h * rows, (h + 1) * rows)
        product = lax.dot_general(low_ref[:, at], keys, ON_TOP, preferred_element_type=F32)
        query_ref[:, h * HEAD : (h + 1) * HEAD] = product.astype(BF16)


def query_gradient(low, vision, rows):
    tokens, pairs = low.shape
    return pl.pallas_call(
        query_kernel,
        out_shape=jax.ShapeDtypeStruct((rows, pairs // rows * HEAD), BF16),
        in_specs=[IN_VMEM] * 2,
        out_specs=IN_VMEM,
        compiler_params=pltpu.CompilerParams(vmem_limit_bytes=32 * 1024 * 1024),
        cost_estimate=pl.CostEstimate(
            flops=2 * pairs * tokens * HEAD, bytes_accessed=2 * pairs * HEAD, transcendentals=0
        ),
        name="query_gradient",
    )(low, vision)


def project_kernel(sums_ref, near_ref, far_ref, cross_ref, *refs):
    weights, (keep_ref, send_ref, grads) = refs[:-3], refs[-3:]
    plane = len(weights)
    me = lax.axis_index("seq")
    core = lax.axis_index("kv")
    home = core == me // (2 * plane)
    odd = lax.rem(me // plane, 2)
    spot = lax.rem(me, plane)
    total = sums_ref[...] + near_ref[...].astype(F32) + far_ref[...].astype(F32)
    grads[...] = (total + cross_ref[...].astype(F32)).astype(BF16)
    first = 2 * core + jnp.where(home, odd, 1 - odd)
    second = 2 * core + jnp.where(home, 1 - odd, odd)
    blocks = [grads[i] for i in (first, second, 3 - first, 3 - second)]
    ordered = jnp.concatenate(blocks, axis=0)
    rows = grads.shape[1]
    for d in range(plane):
        product = lax.dot_general(ordered, weights[d][...], SIDE_BY_SIDE, preferred_element_type=F32)
        columns = weights[d].shape[0]
        at = pl.ds(pl.multiple_of(jnp.bitwise_xor(spot, d) * columns, columns), columns)
        for i in range(2):
            keep_ref[i, :, at] = product[i * rows : (i + 1) * rows]
            send_ref[i, :, at] = product[(i + 2) * rows : (i + 3) * rows].astype(BF16)


def project(sums, arrived, weights):
    rows = sums.shape[1]
    plane = len(weights)
    columns = plane * weights[0].shape[0]
    return pl.pallas_call(
        project_kernel,
        out_shape=(
            jax.ShapeDtypeStruct((2, rows, columns), F32),
            jax.ShapeDtypeStruct((2, rows, columns), BF16),
        ),
        in_specs=[IN_VMEM] * (4 + plane),
        out_specs=(IN_VMEM, IN_VMEM),
        scratch_shapes=[pltpu.VMEM(sums.shape, BF16)],
        compiler_params=pltpu.CompilerParams(vmem_limit_bytes=32 * 1024 * 1024),
        cost_estimate=pl.CostEstimate(
            flops=16 * rows * columns * HEAD, bytes_accessed=4 * columns * HEAD, transcendentals=0
        ),
        name="project",
    )(sums, *arrived, *weights)


def gather_cube(block, cube):
    blocks = [block]
    while len(blocks) < cube:
        distance = len(blocks)
        moved = exchange(jnp.stack(blocks), "seq", 2 * cube, distance)
        blocks += [moved[i] for i in range(distance)]
    return jnp.stack(blocks)


def many_cores(text_query, vision_key, vision_value, grad_output, key_weight, value_weight):
    chips = lax.axis_size("seq")
    cores = lax.axis_size("kv")
    cube = chips // 2
    half = cores // 2
    me = lax.axis_index("seq")
    core = lax.axis_index("kv")
    own = vision_key.shape[0]
    weights = gather_cube(jnp.concatenate([key_weight, value_weight], axis=1), cube)
    vision = lax.all_to_all(spread(vision_key, vision_value, chips), "seq", 0, 0)
    vision = vision.reshape(chips * own, 2 * HEAD)
    low, terms = attention_terms(text_query, grad_output, vision, cube, 2)
    grad_query = query_gradient(low, vision, text_query.shape[0])
    partial = terms[0]
    for d in range(1, cube):
        partial = partial + exchange(terms[d], "seq", chips, d).astype(F32)
    grads = (partial + exchange(partial, "seq", chips, cube)).astype(BF16)
    product = jnp.einsum("qtc,drc->qdtr", grads, weights, preferred_element_type=F32)
    place = (me % cube) ^ jnp.arange(cube)
    product = jnp.take(product, place, axis=1)
    columns = product.transpose(0, 2, 1, 3).reshape(2, own, half, -1).transpose(0, 2, 1, 3)
    columns = columns.reshape(cores, own, -1)
    total = lax.dynamic_index_in_dim(columns, core, 0, keepdims=False)
    for d in range(1, cores):
        other = lax.dynamic_index_in_dim(columns, core ^ d, 0, keepdims=False)
        total = total + exchange(other.astype(BF16), "kv", cores, d).astype(F32)
    total = total.astype(BF16)
    routes = [
        (u * cores + j, (u ^ cube) * cores + (j + half) % cores)
        for u in range(chips)
        for j in range(cores)
        if j // half != u // cube
    ]
    received = lax.ppermute(total, ("seq", "kv"), routes)
    grad_vision = jnp.where(core // half == me // cube, total, received)
    return (grad_query, grad_vision)


def two_cores(text_query, vision_key, vision_value, grad_output, key_weight, value_weight):
    chips = lax.axis_size("seq")
    me = lax.axis_index("seq")
    core = lax.axis_index("kv")
    line = 4
    plane = chips // line
    own = vision_key.shape[0]

    vision = lax.all_to_all(spread(vision_key, vision_value, chips), "seq", 0, 0)
    vision = vision.reshape(chips * own, 2 * HEAD)
    weight = jnp.concatenate([key_weight, value_weight], axis=1)
    weights = [weight] + [exchange(weight, "seq", chips, d) for d in (1, 2)]
    low, terms = attention_terms(text_query, grad_output, vision, plane, line)
    terms, weights = lax.optimization_barrier((terms, weights))
    grad_query = query_gradient(low, vision, text_query.shape[0])
    weight, grad_query = lax.optimization_barrier((weights[0], grad_query))
    weights += [exchange(weight, "seq", chips, d) for d in range(3, plane)]

    arrived = [exchange(terms[d], "seq", chips, d) for d in range(1, plane)]
    arrived, grad_query = lax.optimization_barrier((arrived, grad_query))
    sums = terms[0]
    for block in arrived:
        sums = sums + block.astype(F32)
    near, far, cross = plane, 2 * plane, 3 * plane
    arrived = [exchange(sums.astype(BF16), "seq", chips, d) for d in (near, far, cross)]
    keep, send = project(sums, arrived, weights)
    total = (keep + exchange(send, "kv", 2, 1).astype(F32)).astype(BF16)
    stay, go = total[0], total[1]

    routes_a, routes_b = [], []
    for u in range(chips):
        home = u // far
        routes_a.append((2 * u + home, 2 * (u ^ near) + home))
        routes_a.append((2 * u + 1 - home, 2 * (u ^ far) + home))
        routes_b.append((2 * u + 1 - home, 2 * (u ^ cross) + home))
    at_home = core == me // far
    first = lax.ppermute(go, ("seq", "kv"), routes_a)
    second = lax.ppermute(stay, ("seq", "kv"), routes_b)
    same = jnp.where(at_home, stay, first)
    other = jnp.where(at_home, first, second)
    upper = (me // near) % 2 == 1
    grad_vision = jnp.concatenate(
        [jnp.where(upper, other, same), jnp.where(upper, same, other)], axis=1
    )
    return (grad_query, grad_vision)


def solution(mesh):
    spec = P("seq", "kv")
    return jax.shard_map(
        two_cores if mesh.shape["kv"] == 2 and mesh.shape["seq"] % 4 == 0 else many_cores,
        mesh=mesh,
        in_specs=(spec,) * 6,
        out_specs=(spec, spec),
        check_vma=False,
    )
```

```python
import functools
import math

import jax
import jax.numpy as jnp
from jax import lax
from jax.experimental import pallas as pl
from jax.experimental.pallas import tpu as pltpu
from jax.sharding import PartitionSpec as P

HEAD = 128
F32 = jnp.float32
BF16 = jnp.bfloat16
IN_VMEM = pl.BlockSpec(memory_space=pltpu.VMEM)
SIDE_BY_SIDE = (((1,), (1,)), ((), ()))
ON_TOP = (((0,), (0,)), ((), ()))


def exchange(block, axis, size, distance):
    return lax.ppermute(block, axis, [(i, i ^ distance) for i in range(size)])


def swap(block, chips, distance):
    routes = [(2 * u + c, 2 * (u ^ distance) + 1 - c) for u in range(chips) for c in range(2)]
    return lax.ppermute(block, ("seq", "kv"), routes)


def attention_kernel(line, queries_ref, upstream_ref, *refs):
    vision_refs, low_ref, vision_ref = refs[:line], refs[line], refs[line + 1]
    terms_refs, (rows, low, sums) = refs[line + 2 : -3], refs[-3:]
    for d, ref in enumerate(vision_refs):
        vision_ref[d * ref.shape[0] : (d + 1) * ref.shape[0]] = ref[...]
    row_count, width = queries_ref.shape
    heads = width // HEAD
    scaling = 1.0 / math.sqrt(HEAD)
    keys = vision_ref[:, :HEAD]
    values = vision_ref[:, HEAD:]
    for h in range(heads):
        lanes = slice(h * HEAD, (h + 1) * HEAD)
        at = slice(h * row_count, (h + 1) * row_count)
        rows[0, at, :] = queries_ref[:, lanes]
        rows[1, at, :] = upstream_ref[:, lanes]
    step = 2 if heads % 2 == 0 else 1
    for h in range(0, heads, step):
        at = slice(h * row_count, (h + step) * row_count)
        logits = lax.dot_general(keys, rows[0, at, :], SIDE_BY_SIDE, preferred_element_type=F32)
        grad_probs = lax.dot_general(values, rows[1, at, :], SIDE_BY_SIDE, preferred_element_type=F32)
        top = jnp.max(logits, axis=0, keepdims=True)
        exponent = jnp.exp2((logits - top) * (scaling * math.log2(math.e)))
        inverse = 1.0 / jnp.sum(exponent, axis=0, keepdims=True)
        row_dots = jnp.sum(exponent * grad_probs, axis=0, keepdims=True) * inverse
        low[:, at] = (exponent * inverse).astype(BF16)
        low_ref[:, at] = (exponent * (grad_probs - row_dots) * (inverse * scaling)).astype(BF16)
    _, plane, own, _ = sums.shape
    for i, factor in enumerate((low_ref, low)):
        term = jnp.dot(factor[...], rows[i], preferred_element_type=F32)
        sums[:, :, :, i * HEAD : (i + 1) * HEAD] = term.reshape(line, plane, own, HEAD)
    spot = lax.axis_index("seq") // plane
    for d, ref in enumerate(terms_refs):
        for i in range(line):
            ref[i] = sums[jnp.bitwise_xor(spot, i), d].astype(ref.dtype)


def attention_terms(queries, upstream, blocks, plane):
    rows, width = queries.shape
    line = len(blocks)
    tokens = line * blocks[0].shape[0]
    pairs = rows * width // HEAD
    own = tokens // (plane * line)
    low, vision, *terms = pl.pallas_call(
        functools.partial(attention_kernel, line),
        out_shape=[
            jax.ShapeDtypeStruct((tokens, pairs), BF16),
            jax.ShapeDtypeStruct((tokens, 2 * HEAD), BF16),
        ]
        + [
            jax.ShapeDtypeStruct((line, own, 2 * HEAD), BF16 if d else F32) for d in range(plane)
        ],
        in_specs=[IN_VMEM] * (2 + line),
        out_specs=[IN_VMEM] * (2 + plane),
        scratch_shapes=[
            pltpu.VMEM((2, pairs, HEAD), BF16),
            pltpu.VMEM((tokens, pairs), BF16),
            pltpu.VMEM((line, plane, own, 2 * HEAD), F32),
        ],
        compiler_params=pltpu.CompilerParams(vmem_limit_bytes=48 * 1024 * 1024),
        cost_estimate=pl.CostEstimate(
            flops=8 * pairs * tokens * HEAD,
            bytes_accessed=4 * rows * width + 4 * tokens * HEAD,
            transcendentals=pairs * tokens,
        ),
        name="attention_terms",
    )(queries, upstream, *blocks)
    return low, vision, terms


def query_kernel(low_ref, vision_ref, query_ref):
    rows = query_ref.shape[0]
    keys = vision_ref[:, :HEAD]
    for h in range(query_ref.shape[1] // HEAD):
        at = slice(h * rows, (h + 1) * rows)
        product = lax.dot_general(low_ref[:, at], keys, ON_TOP, preferred_element_type=F32)
        query_ref[:, h * HEAD : (h + 1) * HEAD] = product.astype(BF16)


def query_gradient(low, vision, rows):
    tokens, pairs = low.shape
    return pl.pallas_call(
        query_kernel,
        out_shape=jax.ShapeDtypeStruct((rows, pairs // rows * HEAD), BF16),
        in_specs=[IN_VMEM] * 2,
        out_specs=IN_VMEM,
        compiler_params=pltpu.CompilerParams(vmem_limit_bytes=32 * 1024 * 1024),
        cost_estimate=pl.CostEstimate(
            flops=2 * pairs * tokens * HEAD, bytes_accessed=2 * pairs * HEAD, transcendentals=0
        ),
        name="query_gradient",
    )(low, vision)


def project_kernel(sums_ref, *refs):
    arrived, weights, (keep_ref, send_ref, grads) = refs[:3], refs[3:-3], refs[-3:]
    plane = len(weights)
    me = lax.axis_index("seq")
    core = lax.axis_index("kv")
    home = core == me // (2 * plane)
    odd = lax.rem(me // plane, 2)
    spot = lax.rem(me, plane)
    total = sums_ref[...]
    for ref in arrived:
        total = total + ref[...].astype(F32)
    grads[...] = total.astype(BF16)
    first = 2 * core + jnp.where(home, odd, 1 - odd)
    second = 2 * core + jnp.where(home, 1 - odd, odd)
    blocks = [grads[i] for i in (first, second, 3 - first, 3 - second)]
    ordered = jnp.concatenate(blocks, axis=0)
    rows = grads.shape[1]
    for d in range(plane):
        product = lax.dot_general(ordered, weights[d][...], SIDE_BY_SIDE, preferred_element_type=F32)
        columns = weights[d].shape[0]
        at = pl.ds(pl.multiple_of(jnp.bitwise_xor(spot, d) * columns, columns), columns)
        for i in range(2):
            keep_ref[i, :, at] = product[i * rows : (i + 1) * rows]
            send_ref[i, :, at] = product[(i + 2) * rows : (i + 3) * rows].astype(BF16)


def project(sums, arrived, weights):
    rows = sums.shape[1]
    plane = len(weights)
    columns = plane * weights[0].shape[0]
    return pl.pallas_call(
        project_kernel,
        out_shape=(
            jax.ShapeDtypeStruct((2, rows, columns), F32),
            jax.ShapeDtypeStruct((2, rows, columns), BF16),
        ),
        in_specs=[IN_VMEM] * (4 + plane),
        out_specs=(IN_VMEM, IN_VMEM),
        scratch_shapes=[pltpu.VMEM(sums.shape, BF16)],
        compiler_params=pltpu.CompilerParams(vmem_limit_bytes=32 * 1024 * 1024),
        cost_estimate=pl.CostEstimate(
            flops=16 * rows * columns * HEAD, bytes_accessed=4 * columns * HEAD, transcendentals=0
        ),
        name="project",
    )(sums, *arrived, *weights)


def gather_cube(block, cube):
    blocks = [block]
    while len(blocks) < cube:
        distance = len(blocks)
        moved = exchange(jnp.stack(blocks), "seq", 2 * cube, distance)
        blocks += [moved[i] for i in range(distance)]
    return jnp.stack(blocks)


def many_cores(text_query, vision_key, vision_value, grad_output, key_weight, value_weight):
    chips = lax.axis_size("seq")
    cores = lax.axis_size("kv")
    cube = chips // 2
    half = cores // 2
    me = lax.axis_index("seq")
    core = lax.axis_index("kv")
    own = vision_key.shape[0]
    weights = gather_cube(jnp.concatenate([key_weight, value_weight], axis=1), cube)
    pair = jnp.concatenate([vision_key, vision_value], axis=1)
    block = gather_cube(pair, cube).reshape(cube * own, 2 * HEAD)
    blocks = [block, exchange(block, "seq", chips, cube)]
    low, vision, terms = attention_terms(text_query, grad_output, blocks, cube)
    grad_query = query_gradient(low, vision, text_query.shape[0])
    partial = terms[0]
    for d in range(1, cube):
        partial = partial + exchange(terms[d], "seq", chips, d).astype(F32)
    grads = (partial + exchange(partial, "seq", chips, cube)).astype(BF16)
    product = jnp.einsum("qtc,drc->qdtr", grads, weights, preferred_element_type=F32)
    place = (me % cube) ^ jnp.arange(cube)
    product = jnp.take(product, place, axis=1)
    columns = product.transpose(0, 2, 1, 3).reshape(2, own, half, -1).transpose(0, 2, 1, 3)
    columns = columns.reshape(cores, own, -1)
    total = lax.dynamic_index_in_dim(columns, core, 0, keepdims=False)
    for d in range(1, cores):
        other = lax.dynamic_index_in_dim(columns, core ^ d, 0, keepdims=False)
        total = total + exchange(other.astype(BF16), "kv", cores, d).astype(F32)
    total = total.astype(BF16)
    routes = [
        (u * cores + j, (u ^ cube) * cores + (j + half) % cores)
        for u in range(chips)
        for j in range(cores)
        if j // half != u // cube
    ]
    received = lax.ppermute(total, ("seq", "kv"), routes)
    grad_vision = jnp.where(core // half == me // cube, total, received)
    return (grad_query, grad_vision)


def two_cores(text_query, vision_key, vision_value, grad_output, key_weight, value_weight):
    chips = lax.axis_size("seq")
    me = lax.axis_index("seq")
    core = lax.axis_index("kv")
    line = 4
    plane = chips // line
    own = vision_key.shape[0]

    near, far, cross = plane, 2 * plane, 3 * plane
    pair = jnp.concatenate([vision_key, vision_value], axis=1)
    arrived = {d: swap(pair, chips, d) for d in (3, 1, 2, 0)}
    block = jnp.concatenate([arrived[d] for d in range(plane)], axis=0)
    blocks = {d: swap(block, chips, d) for d in (cross, far, near, 0)}
    weight = jnp.concatenate([key_weight, value_weight], axis=1)
    weights = [weight] + [exchange(weight, "seq", chips, d) for d in (1, 2)]
    low, vision, terms = attention_terms(
        text_query, grad_output, [blocks[d] for d in (0, near, far, cross)], plane
    )
    terms, weights = lax.optimization_barrier((terms, weights))
    grad_query = query_gradient(low, vision, text_query.shape[0])
    weight, grad_query = lax.optimization_barrier((weights[0], grad_query))
    weights += [exchange(weight, "seq", chips, d) for d in range(3, plane)]

    arrived = [exchange(terms[d], "seq", chips, d) for d in range(1, plane)]
    arrived, grad_query = lax.optimization_barrier((arrived, grad_query))
    sums = terms[0]
    for block in arrived:
        sums = sums + block.astype(F32)
    arrived = [exchange(sums.astype(BF16), "seq", chips, d) for d in (cross, far, near)]
    keep, send = project(sums, arrived, weights)
    total = (keep + exchange(send, "kv", 2, 1).astype(F32)).astype(BF16)
    stay, go = total[0], total[1]

    routes_a, routes_b = [], []
    for u in range(chips):
        home = u // far
        routes_a.append((2 * u + home, 2 * (u ^ near) + home))
        routes_a.append((2 * u + 1 - home, 2 * (u ^ far) + home))
        routes_b.append((2 * u + 1 - home, 2 * (u ^ cross) + home))
        routes_b.append((2 * u + home, 2 * (u ^ 1) + home))
    at_home = core == me // far
    first = lax.ppermute(go, ("seq", "kv"), routes_a)
    second = lax.ppermute(stay, ("seq", "kv"), routes_b)
    same = jnp.where(at_home, stay, first)
    other = jnp.where(at_home, first, second)
    upper = (me // near) % 2 == 1
    grad_vision = jnp.concatenate(
        [jnp.where(upper, other, same), jnp.where(upper, same, other)], axis=1
    )
    return (grad_query, grad_vision)


def solution(mesh):
    spec = P("seq", "kv")
    return jax.shard_map(
        two_cores if (mesh.shape["seq"], mesh.shape["kv"]) == (16, 2) else many_cores,
        mesh=mesh,
        in_specs=(spec,) * 6,
        out_specs=(spec, spec),
        check_vma=False,
    )
```

```python
import functools
import math

import jax
import jax.numpy as jnp
from jax import lax
from jax.experimental import pallas as pl
from jax.experimental.pallas import tpu as pltpu
from jax.sharding import PartitionSpec as P

HEAD = 128
F32 = jnp.float32
BF16 = jnp.bfloat16
IN_VMEM = pl.BlockSpec(memory_space=pltpu.VMEM)
SIDE_BY_SIDE = (((1,), (1,)), ((), ()))
ON_TOP = (((0,), (0,)), ((), ()))


def exchange(block, axis, size, distance):
    return lax.ppermute(block, axis, [(i, i ^ distance) for i in range(size)])


def swap(block, chips, distance):
    routes = [(2 * u + c, 2 * (u ^ distance) + 1 - c) for u in range(chips) for c in range(2)]
    return lax.ppermute(block, ("seq", "kv"), routes)


def attention_kernel(outer, queries_ref, upstream_ref, *refs):
    vision_refs, low_ref, vision_ref = refs[:outer], refs[outer], refs[outer + 1]
    terms_refs, (rows, low, sums) = refs[outer + 2 : -3], refs[-3:]
    for d, ref in enumerate(vision_refs):
        vision_ref[d * ref.shape[0] : (d + 1) * ref.shape[0]] = ref[...]
    row_count, width = queries_ref.shape
    heads = width // HEAD
    scaling = 1.0 / math.sqrt(HEAD)
    keys = vision_ref[:, :HEAD]
    values = vision_ref[:, HEAD:]
    for h in range(heads):
        lanes = slice(h * HEAD, (h + 1) * HEAD)
        at = slice(h * row_count, (h + 1) * row_count)
        rows[0, at, :] = queries_ref[:, lanes]
        rows[1, at, :] = upstream_ref[:, lanes]
    step = 2 if heads % 2 == 0 else 1
    for h in range(0, heads, step):
        at = slice(h * row_count, (h + step) * row_count)
        logits = lax.dot_general(keys, rows[0, at, :], SIDE_BY_SIDE, preferred_element_type=F32)
        grad_probs = lax.dot_general(values, rows[1, at, :], SIDE_BY_SIDE, preferred_element_type=F32)
        top = jnp.max(logits, axis=0, keepdims=True)
        exponent = jnp.exp2((logits - top) * (scaling * math.log2(math.e)))
        inverse = 1.0 / jnp.sum(exponent, axis=0, keepdims=True)
        row_dots = jnp.sum(exponent * grad_probs, axis=0, keepdims=True) * inverse
        low[:, at] = (exponent * inverse).astype(BF16)
        low_ref[:, at] = (exponent * (grad_probs - row_dots) * (inverse * scaling)).astype(BF16)
    _, inner, own, _ = sums.shape
    for i, factor in enumerate((low_ref, low)):
        term = jnp.dot(factor[...], rows[i], preferred_element_type=F32)
        sums[:, :, :, i * HEAD : (i + 1) * HEAD] = term.reshape(outer, inner, own, HEAD)
    spot = lax.axis_index("seq") // outer
    for d, ref in enumerate(terms_refs):
        for i in range(inner):
            ref[i] = sums[d, jnp.bitwise_xor(spot, i)].astype(ref.dtype)


def attention_terms(queries, upstream, blocks, inner):
    rows, width = queries.shape
    outer = len(blocks)
    tokens = outer * blocks[0].shape[0]
    pairs = rows * width // HEAD
    own = tokens // (inner * outer)
    low, vision, *terms = pl.pallas_call(
        functools.partial(attention_kernel, outer),
        out_shape=[
            jax.ShapeDtypeStruct((tokens, pairs), BF16),
            jax.ShapeDtypeStruct((tokens, 2 * HEAD), BF16),
        ]
        + [
            jax.ShapeDtypeStruct((inner, own, 2 * HEAD), BF16 if d else F32) for d in range(outer)
        ],
        in_specs=[IN_VMEM] * (2 + outer),
        out_specs=[IN_VMEM] * (2 + outer),
        scratch_shapes=[
            pltpu.VMEM((2, pairs, HEAD), BF16),
            pltpu.VMEM((tokens, pairs), BF16),
            pltpu.VMEM((outer, inner, own, 2 * HEAD), F32),
        ],
        compiler_params=pltpu.CompilerParams(vmem_limit_bytes=48 * 1024 * 1024),
        cost_estimate=pl.CostEstimate(
            flops=40 * pairs * tokens * HEAD,
            bytes_accessed=4 * rows * width + 4 * tokens * HEAD,
            transcendentals=5 * pairs * tokens,
        ),
        name="attention_terms",
    )(queries, upstream, *blocks)
    return low, vision, terms


def query_kernel(low_ref, vision_ref, query_ref):
    rows = query_ref.shape[0]
    keys = vision_ref[:, :HEAD]
    for h in range(query_ref.shape[1] // HEAD):
        at = slice(h * rows, (h + 1) * rows)
        product = lax.dot_general(low_ref[:, at], keys, ON_TOP, preferred_element_type=F32)
        query_ref[:, h * HEAD : (h + 1) * HEAD] = product.astype(BF16)


def query_gradient(low, vision, rows):
    tokens, pairs = low.shape
    return pl.pallas_call(
        query_kernel,
        out_shape=jax.ShapeDtypeStruct((rows, pairs // rows * HEAD), BF16),
        in_specs=[IN_VMEM] * 2,
        out_specs=IN_VMEM,
        compiler_params=pltpu.CompilerParams(vmem_limit_bytes=32 * 1024 * 1024),
        cost_estimate=pl.CostEstimate(
            flops=2 * pairs * tokens * HEAD, bytes_accessed=2 * pairs * HEAD, transcendentals=0
        ),
        name="query_gradient",
    )(low, vision)


def project_kernel(sums_ref, *refs):
    arrived, weights, (keep_ref, send_ref, grads) = refs[:3], refs[3:-3], refs[-3:]
    plane = len(weights)
    me = lax.axis_index("seq")
    core = lax.axis_index("kv")
    home = core == me // (2 * plane)
    odd = lax.rem(me // plane, 2)
    spot = lax.rem(me, plane)
    total = sums_ref[...]
    for ref in arrived:
        total = total + ref[...].astype(F32)
    grads[...] = total.astype(BF16)
    first = 2 * core + jnp.where(home, odd, 1 - odd)
    second = 2 * core + jnp.where(home, 1 - odd, odd)
    blocks = [grads[i] for i in (first, second, 3 - first, 3 - second)]
    ordered = jnp.concatenate(blocks, axis=0)
    rows = grads.shape[1]
    for d in range(plane):
        product = lax.dot_general(ordered, weights[d][...], SIDE_BY_SIDE, preferred_element_type=F32)
        columns = weights[d].shape[0]
        at = pl.ds(pl.multiple_of(jnp.bitwise_xor(spot, d) * columns, columns), columns)
        for i in range(2):
            keep_ref[i, :, at] = product[i * rows : (i + 1) * rows]
            send_ref[i, :, at] = product[(i + 2) * rows : (i + 3) * rows].astype(BF16)


def project(sums, arrived, weights):
    rows = sums.shape[1]
    plane = len(weights)
    columns = plane * weights[0].shape[0]
    return pl.pallas_call(
        project_kernel,
        out_shape=(
            jax.ShapeDtypeStruct((2, rows, columns), F32),
            jax.ShapeDtypeStruct((2, rows, columns), BF16),
        ),
        in_specs=[IN_VMEM] * (4 + plane),
        out_specs=(IN_VMEM, IN_VMEM),
        scratch_shapes=[pltpu.VMEM(sums.shape, BF16)],
        compiler_params=pltpu.CompilerParams(vmem_limit_bytes=32 * 1024 * 1024),
        cost_estimate=pl.CostEstimate(
            flops=16 * rows * columns * HEAD, bytes_accessed=4 * columns * HEAD, transcendentals=0
        ),
        name="project",
    )(sums, *arrived, *weights)


def gather_cube(block, cube):
    blocks = [block]
    while len(blocks) < cube:
        distance = len(blocks)
        moved = exchange(jnp.stack(blocks), "seq", 2 * cube, distance)
        blocks += [moved[i] for i in range(distance)]
    return jnp.stack(blocks)


def many_cores(text_query, vision_key, vision_value, grad_output, key_weight, value_weight):
    chips = lax.axis_size("seq")
    cores = lax.axis_size("kv")
    cube = chips // 2
    half = cores // 2
    me = lax.axis_index("seq")
    core = lax.axis_index("kv")
    own = vision_key.shape[0]
    weights = gather_cube(jnp.concatenate([key_weight, value_weight], axis=1), cube)
    pair = jnp.concatenate([vision_key, vision_value], axis=1)
    both = jnp.concatenate([pair, exchange(pair, "seq", chips, cube)], axis=0)
    blocks = gather_cube(both, cube)
    blocks = [blocks[d] for d in range(cube)]
    low, vision, terms = attention_terms(text_query, grad_output, blocks, 2)
    grad_query = query_gradient(low, vision, text_query.shape[0])
    partial = terms[0]
    for d in range(1, cube):
        partial = partial + exchange(terms[d], "seq", chips, d).astype(F32)
    grads = (partial + exchange(partial, "seq", chips, cube)).astype(BF16)
    product = jnp.einsum("qtc,drc->qdtr", grads, weights, preferred_element_type=F32)
    place = (me % cube) ^ jnp.arange(cube)
    product = jnp.take(product, place, axis=1)
    columns = product.transpose(0, 2, 1, 3).reshape(2, own, half, -1).transpose(0, 2, 1, 3)
    columns = columns.reshape(cores, own, -1)
    total = lax.dynamic_index_in_dim(columns, core, 0, keepdims=False)
    for d in range(1, cores):
        other = lax.dynamic_index_in_dim(columns, core ^ d, 0, keepdims=False)
        total = total + exchange(other.astype(BF16), "kv", cores, d).astype(F32)
    total = total.astype(BF16)
    routes = [
        (u * cores + j, (u ^ cube) * cores + (j + half) % cores)
        for u in range(chips)
        for j in range(cores)
        if j // half != u // cube
    ]
    received = lax.ppermute(total, ("seq", "kv"), routes)
    grad_vision = jnp.where(core // half == me // cube, total, received)
    return (grad_query, grad_vision)


def two_cores(text_query, vision_key, vision_value, grad_output, key_weight, value_weight):
    chips = lax.axis_size("seq")
    me = lax.axis_index("seq")
    core = lax.axis_index("kv")
    line = 4
    plane = chips // line
    own = vision_key.shape[0]

    near, far, cross = plane, 2 * plane, 3 * plane

    pair = jnp.concatenate([vision_key, vision_value], axis=1)
    arrived = {d: swap(pair, chips, d) for d in (cross, far, near, 0)}
    block = jnp.concatenate([arrived[d] for d in (0, near, far, cross)], axis=0)
    blocks = {d: swap(block, chips, d) for d in (3, 1, 2, 0)}
    weight = jnp.concatenate([key_weight, value_weight], axis=1)
    weights = [weight] + [exchange(weight, "seq", chips, d) for d in (1, 2)]
    low, vision, terms = attention_terms(
        text_query, grad_output, [blocks[d] for d in range(plane)], line
    )
    grad_query = query_gradient(low, vision, text_query.shape[0])
    weight, grad_query = lax.optimization_barrier((weight, grad_query))
    weights += [exchange(weight, "seq", chips, d) for d in range(3, plane)]

    arrived = [exchange(terms[d], "seq", chips, d) for d in range(1, plane)]
    arrived, grad_query, weights[1:3] = lax.optimization_barrier((arrived, grad_query, weights[1:3]))
    sums = terms[0]
    for block in arrived:
        sums = sums + block.astype(F32)
    arrived = [exchange(sums.astype(BF16), "seq", chips, d) for d in (far, cross, near)]
    keep, send = project(sums, arrived, weights)
    total = (keep + exchange(send, "kv", 2, 1).astype(F32)).astype(BF16)
    stay, go = total[0], total[1]

    routes_a, routes_b = [], []
    for u in range(chips):
        home = u // far
        routes_a.append((2 * u + home, 2 * (u ^ near) + home))
        routes_a.append((2 * u + 1 - home, 2 * (u ^ far) + home))
        routes_b.append((2 * u + 1 - home, 2 * (u ^ cross) + home))
        routes_b.append((2 * u + home, 2 * (u ^ 1) + home))
    at_home = core == me // far
    first = lax.ppermute(go, ("seq", "kv"), routes_a)
    second = lax.ppermute(stay, ("seq", "kv"), routes_b)
    same = jnp.where(at_home, stay, first)
    other = jnp.where(at_home, first, second)
    upper = (me // near) % 2 == 1
    grad_vision = jnp.concatenate(
        [jnp.where(upper, other, same), jnp.where(upper, same, other)], axis=1
    )
    return (grad_query, grad_vision)


def solution(mesh):
    spec = P("seq", "kv")
    return jax.shard_map(
        two_cores if (mesh.shape["seq"], mesh.shape["kv"]) == (16, 2) else many_cores,
        mesh=mesh,
        in_specs=(spec,) * 6,
        out_specs=(spec, spec),
        check_vma=False,
    )
```

```python
import functools
import math

import jax
import jax.numpy as jnp
from jax import lax
from jax.experimental import pallas as pl
from jax.experimental.pallas import tpu as pltpu
from jax.sharding import PartitionSpec as P

HEAD = 128
F32 = jnp.float32
BF16 = jnp.bfloat16
IN_VMEM = pl.BlockSpec(memory_space=pltpu.VMEM)
SIDE_BY_SIDE = (((1,), (1,)), ((), ()))
ON_TOP = (((0,), (0,)), ((), ()))


def exchange(block, axis, size, distance):
    return lax.ppermute(block, axis, [(i, i ^ distance) for i in range(size)])


def swap(block, chips, distance):
    routes = [(2 * u + c, 2 * (u ^ distance) + 1 - c) for u in range(chips) for c in range(2)]
    return lax.ppermute(block, ("seq", "kv"), routes)


def attention_kernel(outer, queries_ref, upstream_ref, *refs):
    vision_refs, low_ref, vision_ref = refs[:outer], refs[outer], refs[outer + 1]
    terms_refs, (rows, low, sums) = refs[outer + 2 : -3], refs[-3:]
    for d, ref in enumerate(vision_refs):
        vision_ref[d * ref.shape[0] : (d + 1) * ref.shape[0]] = ref[...]
    row_count, width = queries_ref.shape
    heads = width // HEAD
    scaling = 1.0 / math.sqrt(HEAD)
    keys = vision_ref[:, :HEAD]
    values = vision_ref[:, HEAD:]
    for h in range(heads):
        lanes = slice(h * HEAD, (h + 1) * HEAD)
        at = slice(h * row_count, (h + 1) * row_count)
        rows[0, at, :] = queries_ref[:, lanes]
        rows[1, at, :] = upstream_ref[:, lanes]
    step = 2 if heads % 2 == 0 else 1
    for h in range(0, heads, step):
        at = slice(h * row_count, (h + step) * row_count)
        logits = lax.dot_general(keys, rows[0, at, :], SIDE_BY_SIDE, preferred_element_type=F32)
        grad_probs = lax.dot_general(values, rows[1, at, :], SIDE_BY_SIDE, preferred_element_type=F32)
        top = jnp.max(logits, axis=0, keepdims=True)
        exponent = jnp.exp2((logits - top) * (scaling * math.log2(math.e)))
        inverse = 1.0 / jnp.sum(exponent, axis=0, keepdims=True)
        row_dots = jnp.sum(exponent * grad_probs, axis=0, keepdims=True) * inverse
        low[:, at] = (exponent * inverse).astype(BF16)
        low_ref[:, at] = (exponent * (grad_probs - row_dots) * (inverse * scaling)).astype(BF16)
    _, inner, own, _ = sums.shape
    for i, factor in enumerate((low_ref, low)):
        term = jnp.dot(factor[...], rows[i], preferred_element_type=F32)
        sums[:, :, :, i * HEAD : (i + 1) * HEAD] = term.reshape(outer, inner, own, HEAD)
    spot = lax.axis_index("seq") // outer
    for d, ref in enumerate(terms_refs):
        for i in range(inner):
            ref[i] = sums[outer - 1 - d, jnp.bitwise_xor(spot, i)].astype(ref.dtype)


def attention_terms(queries, upstream, blocks, inner):
    rows, width = queries.shape
    outer = len(blocks)
    tokens = outer * blocks[0].shape[0]
    pairs = rows * width // HEAD
    own = tokens // (inner * outer)
    low, vision, *terms = pl.pallas_call(
        functools.partial(attention_kernel, outer),
        out_shape=[
            jax.ShapeDtypeStruct((tokens, pairs), BF16),
            jax.ShapeDtypeStruct((tokens, 2 * HEAD), BF16),
        ]
        + [
            jax.ShapeDtypeStruct((inner, own, 2 * HEAD), BF16 if d else F32) for d in range(outer)
        ],
        in_specs=[IN_VMEM] * (2 + outer),
        out_specs=[IN_VMEM] * (2 + outer),
        scratch_shapes=[
            pltpu.VMEM((2, pairs, HEAD), BF16),
            pltpu.VMEM((tokens, pairs), BF16),
            pltpu.VMEM((outer, inner, own, 2 * HEAD), F32),
        ],
        compiler_params=pltpu.CompilerParams(vmem_limit_bytes=48 * 1024 * 1024),
        cost_estimate=pl.CostEstimate(
            flops=40 * pairs * tokens * HEAD,
            bytes_accessed=4 * rows * width + 4 * tokens * HEAD,
            transcendentals=5 * pairs * tokens,
        ),
        name="attention_terms",
    )(queries, upstream, *blocks)
    return low, vision, terms


def query_kernel(low_ref, vision_ref, query_ref):
    rows = query_ref.shape[0]
    keys = vision_ref[:, :HEAD]
    for h in range(query_ref.shape[1] // HEAD):
        at = slice(h * rows, (h + 1) * rows)
        product = lax.dot_general(low_ref[:, at], keys, ON_TOP, preferred_element_type=F32)
        query_ref[:, h * HEAD : (h + 1) * HEAD] = product.astype(BF16)


def query_gradient(low, vision, rows):
    tokens, pairs = low.shape
    return pl.pallas_call(
        query_kernel,
        out_shape=jax.ShapeDtypeStruct((rows, pairs // rows * HEAD), BF16),
        in_specs=[IN_VMEM] * 2,
        out_specs=IN_VMEM,
        compiler_params=pltpu.CompilerParams(vmem_limit_bytes=32 * 1024 * 1024),
        cost_estimate=pl.CostEstimate(
            flops=2 * pairs * tokens * HEAD, bytes_accessed=2 * pairs * HEAD, transcendentals=0
        ),
        name="query_gradient",
    )(low, vision)


def project_kernel(sums_ref, *refs):
    arrived, weights, (keep_ref, send_ref, grads) = refs[:3], refs[3:-3], refs[-3:]
    plane = len(weights)
    me = lax.axis_index("seq")
    core = lax.axis_index("kv")
    home = core == me // (2 * plane)
    odd = lax.rem(me // plane, 2)
    spot = lax.rem(me, plane)
    total = sums_ref[...]
    for ref in arrived:
        total = total + ref[...].astype(F32)
    grads[...] = total.astype(BF16)
    first = 2 * core + jnp.where(home, odd, 1 - odd)
    second = 2 * core + jnp.where(home, 1 - odd, odd)
    blocks = [grads[i] for i in (first, second, 3 - first, 3 - second)]
    ordered = jnp.concatenate(blocks, axis=0)
    rows = grads.shape[1]
    for d in range(plane):
        product = lax.dot_general(ordered, weights[d][...], SIDE_BY_SIDE, preferred_element_type=F32)
        columns = weights[d].shape[0]
        at = pl.ds(pl.multiple_of(jnp.bitwise_xor(spot, d) * columns, columns), columns)
        for i in range(2):
            keep_ref[i, :, at] = product[i * rows : (i + 1) * rows]
            send_ref[i, :, at] = product[(i + 2) * rows : (i + 3) * rows].astype(BF16)


def project(sums, arrived, weights):
    rows = sums.shape[1]
    plane = len(weights)
    columns = plane * weights[0].shape[0]
    return pl.pallas_call(
        project_kernel,
        out_shape=(
            jax.ShapeDtypeStruct((2, rows, columns), F32),
            jax.ShapeDtypeStruct((2, rows, columns), BF16),
        ),
        in_specs=[IN_VMEM] * (4 + plane),
        out_specs=(IN_VMEM, IN_VMEM),
        scratch_shapes=[pltpu.VMEM(sums.shape, BF16)],
        compiler_params=pltpu.CompilerParams(vmem_limit_bytes=32 * 1024 * 1024),
        cost_estimate=pl.CostEstimate(
            flops=16 * rows * columns * HEAD, bytes_accessed=4 * columns * HEAD, transcendentals=0
        ),
        name="project",
    )(sums, *arrived, *weights)


def gather_cube(block, cube):
    blocks = [block]
    while len(blocks) < cube:
        distance = len(blocks)
        moved = exchange(jnp.stack(blocks), "seq", 2 * cube, distance)
        blocks += [moved[i] for i in range(distance)]
    return jnp.stack(blocks)


def many_cores(text_query, vision_key, vision_value, grad_output, key_weight, value_weight):
    chips = lax.axis_size("seq")
    cores = lax.axis_size("kv")
    cube = chips // 2
    half = cores // 2
    me = lax.axis_index("seq")
    core = lax.axis_index("kv")
    own = vision_key.shape[0]
    weights = gather_cube(jnp.concatenate([key_weight, value_weight], axis=1), cube)
    pair = jnp.concatenate([vision_key, vision_value], axis=1)
    both = jnp.concatenate([pair, exchange(pair, "seq", chips, cube)], axis=0)
    blocks = gather_cube(both, cube)
    blocks = [blocks[d] for d in reversed(range(cube))]
    low, vision, terms = attention_terms(text_query, grad_output, blocks, 2)
    grad_query = query_gradient(low, vision, text_query.shape[0])
    partial = terms[0]
    for d in range(1, cube):
        partial = partial + exchange(terms[d], "seq", chips, d).astype(F32)
    grads = (partial + exchange(partial, "seq", chips, cube)).astype(BF16)
    product = jnp.einsum("qtc,drc->qdtr", grads, weights, preferred_element_type=F32)
    place = (me % cube) ^ jnp.arange(cube)
    product = jnp.take(product, place, axis=1)
    columns = product.transpose(0, 2, 1, 3).reshape(2, own, half, -1).transpose(0, 2, 1, 3)
    columns = columns.reshape(cores, own, -1)
    total = lax.dynamic_index_in_dim(columns, core, 0, keepdims=False)
    for d in range(1, cores):
        other = lax.dynamic_index_in_dim(columns, core ^ d, 0, keepdims=False)
        total = total + exchange(other.astype(BF16), "kv", cores, d).astype(F32)
    total = total.astype(BF16)
    routes = [
        (u * cores + j, (u ^ cube) * cores + (j + half) % cores)
        for u in range(chips)
        for j in range(cores)
        if j // half != u // cube
    ]
    received = lax.ppermute(total, ("seq", "kv"), routes)
    grad_vision = jnp.where(core // half == me // cube, total, received)
    return (grad_query, grad_vision)


def two_cores(text_query, vision_key, vision_value, grad_output, key_weight, value_weight):
    chips = lax.axis_size("seq")
    me = lax.axis_index("seq")
    core = lax.axis_index("kv")
    line = 4
    plane = chips // line
    own = vision_key.shape[0]

    near, far, cross = plane, 2 * plane, 3 * plane

    pair = jnp.concatenate([vision_key, vision_value], axis=1)
    arrived = {d: swap(pair, chips, d) for d in (cross, far, near, 0)}
    block = jnp.concatenate([arrived[d] for d in (0, near, far, cross)], axis=0)
    blocks = {d: swap(block, chips, d) for d in (3, 1, 2, 0)}
    weight = jnp.concatenate([key_weight, value_weight], axis=1)
    weights = [weight] + [exchange(weight, "seq", chips, d) for d in (1, 2)]
    low, vision, terms = attention_terms(
        text_query, grad_output, [blocks[d] for d in reversed(range(plane))], line
    )
    grad_query = query_gradient(low, vision, text_query.shape[0])
    weight, grad_query = lax.optimization_barrier((weight, grad_query))
    weights += [exchange(weight, "seq", chips, d) for d in range(3, plane)]

    arrived = [exchange(terms[d], "seq", chips, d) for d in range(1, plane)]
    arrived, grad_query, weights[1:3] = lax.optimization_barrier((arrived, grad_query, weights[1:3]))
    sums = terms[0]
    for block in arrived:
        sums = sums + block.astype(F32)
    arrived = [exchange(sums.astype(BF16), "seq", chips, d) for d in (far, cross, near)]
    keep, send = project(sums, arrived, weights)
    total = (keep + exchange(send, "kv", 2, 1).astype(F32)).astype(BF16)
    stay, go = total[0], total[1]

    routes_a, routes_b = [], []
    for u in range(chips):
        home = u // far
        routes_a.append((2 * u + home, 2 * (u ^ near) + home))
        routes_a.append((2 * u + 1 - home, 2 * (u ^ far) + home))
        routes_b.append((2 * u + 1 - home, 2 * (u ^ cross) + home))
        routes_b.append((2 * u + home, 2 * (u ^ 1) + home))
    at_home = core == me // far
    second = lax.ppermute(stay, ("seq", "kv"), routes_b)
    first = lax.ppermute(go, ("seq", "kv"), routes_a)
    same = jnp.where(at_home, stay, first)
    other = jnp.where(at_home, first, second)
    upper = (me // near) % 2 == 1
    grad_vision = jnp.concatenate(
        [jnp.where(upper, other, same), jnp.where(upper, same, other)], axis=1
    )
    return (grad_query, grad_vision)


def solution(mesh):
    spec = P("seq", "kv")
    return jax.shard_map(
        two_cores if (mesh.shape["seq"], mesh.shape["kv"]) == (16, 2) else many_cores,
        mesh=mesh,
        in_specs=(spec,) * 6,
        out_specs=(spec, spec),
        check_vma=False,
    )
```

```python
import functools
import math

import jax
import jax.numpy as jnp
from jax import lax
from jax.experimental import pallas as pl
from jax.experimental.pallas import tpu as pltpu
from jax.sharding import PartitionSpec as P

HEAD = 128
F32 = jnp.float32
BF16 = jnp.bfloat16
IN_VMEM = pl.BlockSpec(memory_space=pltpu.VMEM)
SIDE_BY_SIDE = (((1,), (1,)), ((), ()))
ON_TOP = (((0,), (0,)), ((), ()))


def exchange(block, axis, size, distance):
    return lax.ppermute(block, axis, [(i, i ^ distance) for i in range(size)])


def swap(block, chips, distance):
    routes = [(2 * u + c, 2 * (u ^ distance) + 1 - c) for u in range(chips) for c in range(2)]
    return lax.ppermute(block, ("seq", "kv"), routes)


def attention_kernel(outer, queries_ref, upstream_ref, *refs):
    vision_refs, low_ref, vision_ref = refs[:outer], refs[outer], refs[outer + 1]
    terms_refs, (rows, low, sums) = refs[outer + 2 : -3], refs[-3:]
    for d, ref in enumerate(vision_refs):
        vision_ref[d * ref.shape[0] : (d + 1) * ref.shape[0]] = ref[...]
    row_count, width = queries_ref.shape
    heads = width // HEAD
    scaling = 1.0 / math.sqrt(HEAD)
    keys = vision_ref[:, :HEAD]
    values = vision_ref[:, HEAD:]
    for h in range(heads):
        lanes = slice(h * HEAD, (h + 1) * HEAD)
        at = slice(h * row_count, (h + 1) * row_count)
        rows[0, at, :] = queries_ref[:, lanes]
        rows[1, at, :] = upstream_ref[:, lanes]
    step = 2 if heads % 2 == 0 else 1
    for h in range(0, heads, step):
        at = slice(h * row_count, (h + step) * row_count)
        logits = lax.dot_general(keys, rows[0, at, :], SIDE_BY_SIDE, preferred_element_type=F32)
        grad_probs = lax.dot_general(values, rows[1, at, :], SIDE_BY_SIDE, preferred_element_type=F32)
        top = jnp.max(logits, axis=0, keepdims=True)
        exponent = jnp.exp2((logits - top) * (scaling * math.log2(math.e)))
        inverse = 1.0 / jnp.sum(exponent, axis=0, keepdims=True)
        row_dots = jnp.sum(exponent * grad_probs, axis=0, keepdims=True) * inverse
        low[:, at] = (exponent * inverse).astype(BF16)
        low_ref[:, at] = (exponent * (grad_probs - row_dots) * (inverse * scaling)).astype(BF16)
    _, inner, own, _ = sums.shape
    for i, factor in enumerate((low_ref, low)):
        term = jnp.dot(factor[...], rows[i], preferred_element_type=F32)
        sums[:, :, :, i * HEAD : (i + 1) * HEAD] = term.reshape(outer, inner, own, HEAD)
    spot = lax.axis_index("seq") // outer
    for d, ref in enumerate(terms_refs):
        for i in range(inner):
            ref[i] = sums[outer - 1 - d, lax.rem(inner - jnp.bitwise_xor(spot, i), inner)].astype(ref.dtype)


def attention_terms(queries, upstream, blocks, inner):
    rows, width = queries.shape
    outer = len(blocks)
    tokens = outer * blocks[0].shape[0]
    pairs = rows * width // HEAD
    own = tokens // (inner * outer)
    low, vision, *terms = pl.pallas_call(
        functools.partial(attention_kernel, outer),
        out_shape=[
            jax.ShapeDtypeStruct((tokens, pairs), BF16),
            jax.ShapeDtypeStruct((tokens, 2 * HEAD), BF16),
        ]
        + [
            jax.ShapeDtypeStruct((inner, own, 2 * HEAD), BF16 if d else F32) for d in range(outer)
        ],
        in_specs=[IN_VMEM] * (2 + outer),
        out_specs=[IN_VMEM] * (2 + outer),
        scratch_shapes=[
            pltpu.VMEM((2, pairs, HEAD), BF16),
            pltpu.VMEM((tokens, pairs), BF16),
            pltpu.VMEM((outer, inner, own, 2 * HEAD), F32),
        ],
        compiler_params=pltpu.CompilerParams(vmem_limit_bytes=48 * 1024 * 1024),
        cost_estimate=pl.CostEstimate(
            flops=40 * pairs * tokens * HEAD,
            bytes_accessed=4 * rows * width + 4 * tokens * HEAD,
            transcendentals=5 * pairs * tokens,
        ),
        name="attention_terms",
    )(queries, upstream, *blocks)
    return low, vision, terms


def query_kernel(low_ref, vision_ref, query_ref):
    rows = query_ref.shape[0]
    keys = vision_ref[:, :HEAD]
    for h in range(query_ref.shape[1] // HEAD):
        at = slice(h * rows, (h + 1) * rows)
        product = lax.dot_general(low_ref[:, at], keys, ON_TOP, preferred_element_type=F32)
        query_ref[:, h * HEAD : (h + 1) * HEAD] = product.astype(BF16)


def query_gradient(low, vision, rows):
    tokens, pairs = low.shape
    return pl.pallas_call(
        query_kernel,
        out_shape=jax.ShapeDtypeStruct((rows, pairs // rows * HEAD), BF16),
        in_specs=[IN_VMEM] * 2,
        out_specs=IN_VMEM,
        compiler_params=pltpu.CompilerParams(vmem_limit_bytes=32 * 1024 * 1024),
        cost_estimate=pl.CostEstimate(
            flops=2 * pairs * tokens * HEAD, bytes_accessed=2 * pairs * HEAD, transcendentals=0
        ),
        name="query_gradient",
    )(low, vision)


def project_kernel(sums_ref, *refs):
    arrived, weights, (keep_ref, send_ref, grads) = refs[:3], refs[3:-3], refs[-3:]
    plane = len(weights)
    me = lax.axis_index("seq")
    core = lax.axis_index("kv")
    home = core == me // (2 * plane)
    odd = lax.rem(me // plane, 2)
    spot = lax.rem(me, plane)
    total = sums_ref[...]
    for ref in arrived:
        total = total + ref[...].astype(F32)
    grads[...] = total.astype(BF16)
    first = 2 * core + jnp.where(home, odd, 1 - odd)
    second = 2 * core + jnp.where(home, 1 - odd, odd)
    blocks = [grads[i] for i in (first, second, 3 - first, 3 - second)]
    ordered = jnp.concatenate(blocks, axis=0)
    rows = grads.shape[1]
    for d in range(plane):
        product = lax.dot_general(ordered, weights[d][...], SIDE_BY_SIDE, preferred_element_type=F32)
        columns = weights[d].shape[0]
        at = pl.ds(pl.multiple_of(jnp.bitwise_xor(spot, d) * columns, columns), columns)
        for i in range(2):
            keep_ref[i, :, at] = product[i * rows : (i + 1) * rows]
            send_ref[i, :, at] = product[(i + 2) * rows : (i + 3) * rows].astype(BF16)


def project(sums, arrived, weights):
    rows = sums.shape[1]
    plane = len(weights)
    columns = plane * weights[0].shape[0]
    return pl.pallas_call(
        project_kernel,
        out_shape=(
            jax.ShapeDtypeStruct((2, rows, columns), F32),
            jax.ShapeDtypeStruct((2, rows, columns), BF16),
        ),
        in_specs=[IN_VMEM] * (4 + plane),
        out_specs=(IN_VMEM, IN_VMEM),
        scratch_shapes=[pltpu.VMEM(sums.shape, BF16)],
        compiler_params=pltpu.CompilerParams(vmem_limit_bytes=32 * 1024 * 1024),
        cost_estimate=pl.CostEstimate(
            flops=16 * rows * columns * HEAD, bytes_accessed=4 * columns * HEAD, transcendentals=0
        ),
        name="project",
    )(sums, *arrived, *weights)


def gather_cube(block, cube):
    blocks = [block]
    while len(blocks) < cube:
        distance = len(blocks)
        moved = exchange(jnp.stack(blocks), "seq", 2 * cube, distance)
        blocks += [moved[i] for i in range(distance)]
    return jnp.stack(blocks)


def many_cores(text_query, vision_key, vision_value, grad_output, key_weight, value_weight):
    chips = lax.axis_size("seq")
    cores = lax.axis_size("kv")
    cube = chips // 2
    half = cores // 2
    me = lax.axis_index("seq")
    core = lax.axis_index("kv")
    own = vision_key.shape[0]
    weights = gather_cube(jnp.concatenate([key_weight, value_weight], axis=1), cube)
    pair = jnp.concatenate([vision_key, vision_value], axis=1)
    both = jnp.concatenate([pair, exchange(pair, "seq", chips, cube)], axis=0)
    blocks = gather_cube(both, cube)
    blocks = [blocks[d] for d in reversed(range(cube))]
    low, vision, terms = attention_terms(text_query, grad_output, blocks, 2)
    grad_query = query_gradient(low, vision, text_query.shape[0])
    partial = terms[0]
    for d in range(1, cube):
        partial = partial + exchange(terms[d], "seq", chips, d).astype(F32)
    grads = (partial + exchange(partial, "seq", chips, cube)).astype(BF16)
    product = jnp.einsum("qtc,drc->qdtr", grads, weights, preferred_element_type=F32)
    place = (me % cube) ^ jnp.arange(cube)
    product = jnp.take(product, place, axis=1)
    columns = product.transpose(0, 2, 1, 3).reshape(2, own, half, -1).transpose(0, 2, 1, 3)
    columns = columns.reshape(cores, own, -1)
    total = lax.dynamic_index_in_dim(columns, core, 0, keepdims=False)
    for d in range(1, cores):
        other = lax.dynamic_index_in_dim(columns, core ^ d, 0, keepdims=False)
        total = total + exchange(other.astype(BF16), "kv", cores, d).astype(F32)
    total = total.astype(BF16)
    routes = [
        (u * cores + j, (u ^ cube) * cores + (j + half) % cores)
        for u in range(chips)
        for j in range(cores)
        if j // half != u // cube
    ]
    received = lax.ppermute(total, ("seq", "kv"), routes)
    grad_vision = jnp.where(core // half == me // cube, total, received)
    return (grad_query, grad_vision)


def two_cores(text_query, vision_key, vision_value, grad_output, key_weight, value_weight):
    chips = lax.axis_size("seq")
    me = lax.axis_index("seq")
    core = lax.axis_index("kv")
    line = 4
    plane = chips // line
    own = vision_key.shape[0]

    near, far, cross = plane, 2 * plane, 3 * plane

    pair = jnp.concatenate([vision_key, vision_value], axis=1)
    arrived = {d: swap(pair, chips, d) for d in (cross, far, near, 0)}
    block = jnp.concatenate([arrived[d] for d in (0, cross, far, near)], axis=0)
    blocks = {d: swap(block, chips, d) for d in (3, 1, 2, 0)}
    weight = jnp.concatenate([key_weight, value_weight], axis=1)
    weights = [weight] + [exchange(weight, "seq", chips, d) for d in (1, 2)]
    low, vision, terms = attention_terms(
        text_query, grad_output, [blocks[d] for d in reversed(range(plane))], line
    )
    grad_query = query_gradient(low, vision, text_query.shape[0])
    weight, grad_query = lax.optimization_barrier((weight, grad_query))
    weights += [exchange(weight, "seq", chips, d) for d in range(3, plane)]

    arrived = [exchange(terms[d], "seq", chips, d) for d in range(1, plane)]
    arrived, grad_query, weights[1:3] = lax.optimization_barrier((arrived, grad_query, weights[1:3]))
    sums = terms[0]
    for block in arrived:
        sums = sums + block.astype(F32)
    arrived = [exchange(sums.astype(BF16), "seq", chips, d) for d in (far, cross, near)]
    keep, send = project(sums, arrived, weights)
    total = (keep + exchange(send, "kv", 2, 1).astype(F32)).astype(BF16)
    stay, go = total[0], total[1]

    routes_a, routes_b = [], []
    for u in range(chips):
        home = u // far
        routes_a.append((2 * u + home, 2 * (u ^ near) + home))
        routes_a.append((2 * u + 1 - home, 2 * (u ^ far) + home))
        routes_b.append((2 * u + 1 - home, 2 * (u ^ cross) + home))
        routes_b.append((2 * u + home, 2 * (u ^ 1) + home))
    at_home = core == me // far
    second = lax.ppermute(stay, ("seq", "kv"), routes_b)
    first = lax.ppermute(go, ("seq", "kv"), routes_a)
    same = jnp.where(at_home, stay, first)
    other = jnp.where(at_home, first, second)
    upper = (me // near) % 2 == 1
    grad_vision = jnp.concatenate(
        [jnp.where(upper, other, same), jnp.where(upper, same, other)], axis=1
    )
    return (grad_query, grad_vision)


def solution(mesh):
    spec = P("seq", "kv")
    return jax.shard_map(
        two_cores if (mesh.shape["seq"], mesh.shape["kv"]) == (16, 2) else many_cores,
        mesh=mesh,
        in_specs=(spec,) * 6,
        out_specs=(spec, spec),
        check_vma=False,
    )
```

```python
import functools
import math

import jax
import jax.numpy as jnp
from jax import lax
from jax.experimental import pallas as pl
from jax.experimental.pallas import tpu as pltpu
from jax.sharding import PartitionSpec as P

HEAD = 128
F32 = jnp.float32
BF16 = jnp.bfloat16
IN_VMEM = pl.BlockSpec(memory_space=pltpu.VMEM)
SIDE_BY_SIDE = (((1,), (1,)), ((), ()))
ON_TOP = (((0,), (0,)), ((), ()))


def exchange(block, axis, size, distance):
    return lax.ppermute(block, axis, [(i, i ^ distance) for i in range(size)])


def swap(block, chips, distance):
    routes = [(2 * u + c, 2 * (u ^ distance) + 1 - c) for u in range(chips) for c in range(2)]
    return lax.ppermute(block, ("seq", "kv"), routes)


def attention_kernel(outer, queries_ref, upstream_ref, *refs):
    vision_refs, low_ref, vision_ref = refs[:outer], refs[outer], refs[outer + 1]
    terms_refs, (rows, low, sums) = refs[outer + 2 : -3], refs[-3:]
    for d, ref in enumerate(vision_refs):
        vision_ref[d * ref.shape[0] : (d + 1) * ref.shape[0]] = ref[...]
    row_count, width = queries_ref.shape
    heads = width // HEAD
    scaling = 1.0 / math.sqrt(HEAD)
    keys = vision_ref[:, :HEAD]
    values = vision_ref[:, HEAD:]
    for h in range(heads):
        lanes = slice(h * HEAD, (h + 1) * HEAD)
        at = slice(h * row_count, (h + 1) * row_count)
        rows[0, at, :] = queries_ref[:, lanes]
        rows[1, at, :] = upstream_ref[:, lanes]
    step = 2 if heads % 2 == 0 else 1
    for h in range(0, heads, step):
        at = slice(h * row_count, (h + step) * row_count)
        logits = lax.dot_general(keys, rows[0, at, :], SIDE_BY_SIDE, preferred_element_type=F32)
        grad_probs = lax.dot_general(values, rows[1, at, :], SIDE_BY_SIDE, preferred_element_type=F32)
        top = jnp.max(logits, axis=0, keepdims=True)
        exponent = jnp.exp2((logits - top) * (scaling * math.log2(math.e)))
        inverse = 1.0 / jnp.sum(exponent, axis=0, keepdims=True)
        row_dots = jnp.sum(exponent * grad_probs, axis=0, keepdims=True) * inverse
        low[:, at] = (exponent * inverse).astype(BF16)
        low_ref[:, at] = (exponent * (grad_probs - row_dots) * (inverse * scaling)).astype(BF16)
    _, inner, own, _ = sums.shape
    for i, factor in enumerate((low_ref, low)):
        term = jnp.dot(factor[...], rows[i], preferred_element_type=F32)
        sums[:, :, :, i * HEAD : (i + 1) * HEAD] = term.reshape(outer, inner, own, HEAD)
    spot = lax.axis_index("seq") // outer
    for d, ref in enumerate(terms_refs):
        for i in range(inner):
            ref[i] = sums[outer - 1 - d, lax.rem(inner - jnp.bitwise_xor(spot, i), inner)].astype(ref.dtype)


def attention_terms(queries, upstream, blocks, inner):
    rows, width = queries.shape
    outer = len(blocks)
    tokens = outer * blocks[0].shape[0]
    pairs = rows * width // HEAD
    own = tokens // (inner * outer)
    low, vision, *terms = pl.pallas_call(
        functools.partial(attention_kernel, outer),
        out_shape=[
            jax.ShapeDtypeStruct((tokens, pairs), BF16),
            jax.ShapeDtypeStruct((tokens, 2 * HEAD), BF16),
        ]
        + [
            jax.ShapeDtypeStruct((inner, own, 2 * HEAD), BF16 if d else F32) for d in range(outer)
        ],
        in_specs=[IN_VMEM] * (2 + outer),
        out_specs=[IN_VMEM] * (2 + outer),
        scratch_shapes=[
            pltpu.VMEM((2, pairs, HEAD), BF16),
            pltpu.VMEM((tokens, pairs), BF16),
            pltpu.VMEM((outer, inner, own, 2 * HEAD), F32),
        ],
        compiler_params=pltpu.CompilerParams(vmem_limit_bytes=48 * 1024 * 1024),
        cost_estimate=pl.CostEstimate(
            flops=40 * pairs * tokens * HEAD,
            bytes_accessed=4 * rows * width + 4 * tokens * HEAD,
            transcendentals=5 * pairs * tokens,
        ),
        name="attention_terms",
    )(queries, upstream, *blocks)
    return low, vision, terms


def query_kernel(low_ref, vision_ref, query_ref):
    rows = query_ref.shape[0]
    keys = vision_ref[:, :HEAD]
    for h in range(query_ref.shape[1] // HEAD):
        at = slice(h * rows, (h + 1) * rows)
        product = lax.dot_general(low_ref[:, at], keys, ON_TOP, preferred_element_type=F32)
        query_ref[:, h * HEAD : (h + 1) * HEAD] = product.astype(BF16)


def query_gradient(low, vision, rows):
    tokens, pairs = low.shape
    return pl.pallas_call(
        query_kernel,
        out_shape=jax.ShapeDtypeStruct((rows, pairs // rows * HEAD), BF16),
        in_specs=[IN_VMEM] * 2,
        out_specs=IN_VMEM,
        compiler_params=pltpu.CompilerParams(vmem_limit_bytes=32 * 1024 * 1024),
        cost_estimate=pl.CostEstimate(
            flops=2 * pairs * tokens * HEAD, bytes_accessed=2 * pairs * HEAD, transcendentals=0
        ),
        name="query_gradient",
    )(low, vision)


def project_kernel(sums_ref, *refs):
    arrived, weights, (keep_ref, send_ref, grads) = refs[:3], refs[3:-3], refs[-3:]
    plane = len(weights)
    me = lax.axis_index("seq")
    core = lax.axis_index("kv")
    home = core == me // (2 * plane)
    odd = lax.rem(me // plane, 2)
    spot = lax.rem(me, plane)
    total = sums_ref[...]
    for ref in arrived:
        total = total + ref[...].astype(F32)
    grads[...] = total.astype(BF16)
    first = 2 * core + jnp.where(home, odd, 1 - odd)
    second = 2 * core + jnp.where(home, 1 - odd, odd)
    blocks = [grads[i] for i in (first, second, 3 - first, 3 - second)]
    ordered = jnp.concatenate(blocks, axis=0)
    rows = grads.shape[1]
    for d in range(plane):
        product = lax.dot_general(ordered, weights[d][...], SIDE_BY_SIDE, preferred_element_type=F32)
        columns = weights[d].shape[0]
        at = pl.ds(pl.multiple_of(jnp.bitwise_xor(spot, d) * columns, columns), columns)
        for i in range(2):
            keep_ref[i, :, at] = product[i * rows : (i + 1) * rows]
            send_ref[i, :, at] = product[(i + 2) * rows : (i + 3) * rows].astype(BF16)


def project(sums, arrived, weights):
    rows = sums.shape[1]
    plane = len(weights)
    columns = plane * weights[0].shape[0]
    return pl.pallas_call(
        project_kernel,
        out_shape=(
            jax.ShapeDtypeStruct((2, rows, columns), F32),
            jax.ShapeDtypeStruct((2, rows, columns), BF16),
        ),
        in_specs=[IN_VMEM] * (4 + plane),
        out_specs=(IN_VMEM, IN_VMEM),
        scratch_shapes=[pltpu.VMEM(sums.shape, BF16)],
        compiler_params=pltpu.CompilerParams(vmem_limit_bytes=32 * 1024 * 1024),
        cost_estimate=pl.CostEstimate(
            flops=16 * rows * columns * HEAD, bytes_accessed=4 * columns * HEAD, transcendentals=0
        ),
        name="project",
    )(sums, *arrived, *weights)


def gather_cube(block, cube):
    blocks = [block]
    while len(blocks) < cube:
        distance = len(blocks)
        moved = exchange(jnp.stack(blocks), "seq", 2 * cube, distance)
        blocks += [moved[i] for i in range(distance)]
    return jnp.stack(blocks)


def many_cores(text_query, vision_key, vision_value, grad_output, key_weight, value_weight):
    chips = lax.axis_size("seq")
    cores = lax.axis_size("kv")
    cube = chips // 2
    half = cores // 2
    me = lax.axis_index("seq")
    core = lax.axis_index("kv")
    own = vision_key.shape[0]
    weights = gather_cube(jnp.concatenate([key_weight, value_weight], axis=1), cube)
    pair = jnp.concatenate([vision_key, vision_value], axis=1)
    both = jnp.concatenate([pair, exchange(pair, "seq", chips, cube)], axis=0)
    blocks = gather_cube(both, cube)
    blocks = [blocks[d] for d in reversed(range(cube))]
    low, vision, terms = attention_terms(text_query, grad_output, blocks, 2)
    grad_query = query_gradient(low, vision, text_query.shape[0])
    partial = terms[0]
    for d in range(1, cube):
        partial = partial + exchange(terms[d], "seq", chips, d).astype(F32)
    grads = (partial + exchange(partial, "seq", chips, cube)).astype(BF16)
    product = jnp.einsum("qtc,drc->qdtr", grads, weights, preferred_element_type=F32)
    place = (me % cube) ^ jnp.arange(cube)
    product = jnp.take(product, place, axis=1)
    columns = product.transpose(0, 2, 1, 3).reshape(2, own, half, -1).transpose(0, 2, 1, 3)
    columns = columns.reshape(cores, own, -1)
    total = lax.dynamic_index_in_dim(columns, core, 0, keepdims=False)
    for d in range(1, cores):
        other = lax.dynamic_index_in_dim(columns, core ^ d, 0, keepdims=False)
        total = total + exchange(other.astype(BF16), "kv", cores, d).astype(F32)
    total = total.astype(BF16)
    routes = [
        (u * cores + j, (u ^ cube) * cores + (j + half) % cores)
        for u in range(chips)
        for j in range(cores)
        if j // half != u // cube
    ]
    received = lax.ppermute(total, ("seq", "kv"), routes)
    grad_vision = jnp.where(core // half == me // cube, total, received)
    return (grad_query, grad_vision)


def two_cores(text_query, vision_key, vision_value, grad_output, key_weight, value_weight):
    chips = lax.axis_size("seq")
    me = lax.axis_index("seq")
    core = lax.axis_index("kv")
    line = 4
    plane = chips // line
    own = vision_key.shape[0]

    near, far, cross = plane, 2 * plane, 3 * plane

    pair = jnp.concatenate([vision_key, vision_value], axis=1)
    arrived = {d: swap(pair, chips, d) for d in (cross, far, near, 0)}
    block = jnp.concatenate([arrived[d] for d in (0, cross, far, near)], axis=0)
    blocks = {d: swap(block, chips, d) for d in (3, 1, 2, 0)}
    weight = jnp.concatenate([key_weight, value_weight], axis=1)
    weights = [exchange(weight, "seq", chips, d) for d in (2, 1)]
    weights = [weight, weights[1], weights[0]]
    low, vision, terms = attention_terms(
        text_query, grad_output, [blocks[d] for d in reversed(range(plane))], line
    )
    grad_query = query_gradient(low, vision, text_query.shape[0])
    weight, grad_query = lax.optimization_barrier((weight, grad_query))
    weights += [exchange(weight, "seq", chips, d) for d in range(3, plane)]

    arrived = [exchange(terms[d], "seq", chips, d) for d in range(1, plane)]
    arrived, grad_query, weights[1:3] = lax.optimization_barrier((arrived, grad_query, weights[1:3]))
    sums = terms[0]
    for block in arrived:
        sums = sums + block.astype(F32)
    arrived = [exchange(sums.astype(BF16), "seq", chips, d) for d in (far, cross, near)]
    keep, send = project(sums, arrived, weights)
    total = (keep + exchange(send, "kv", 2, 1).astype(F32)).astype(BF16)
    stay, go = total[0], total[1]

    routes_a, routes_b = [], []
    for u in range(chips):
        home = u // far
        routes_a.append((2 * u + home, 2 * (u ^ near) + home))
        routes_a.append((2 * u + 1 - home, 2 * (u ^ far) + home))
        routes_b.append((2 * u + 1 - home, 2 * (u ^ cross) + home))
        routes_b.append((2 * u + home, 2 * (u ^ 1) + home))
    at_home = core == me // far
    second = lax.ppermute(stay, ("seq", "kv"), routes_b)
    first = lax.ppermute(go, ("seq", "kv"), routes_a)
    same = jnp.where(at_home, stay, first)
    other = jnp.where(at_home, first, second)
    upper = (me // near) % 2 == 1
    grad_vision = jnp.concatenate(
        [jnp.where(upper, other, same), jnp.where(upper, same, other)], axis=1
    )
    return (grad_query, grad_vision)


def solution(mesh):
    spec = P("seq", "kv")
    return jax.shard_map(
        two_cores if (mesh.shape["seq"], mesh.shape["kv"]) == (16, 2) else many_cores,
        mesh=mesh,
        in_specs=(spec,) * 6,
        out_specs=(spec, spec),
        check_vma=False,
    )
```
